32 devices in a mesh: gx: 2 (over x), gy: 4 (over z), gz: 4 (over y, core).
Axes of the slice: x: 2, y: 2, z: 4, core: 2. Of those that a mesh axis runs over, the one named last changes fastest.
Arguments:
- snapshots: float32 [4, 4, 4096, 8192], P(None, 'gz', 'gx', 'gy'), may hold values from -6 to 6
- steps: int32 [4], replicated, may hold values from 0 to 3999
- mask: int32 [4, 64], replicated, may hold values 0 or 1
- probe: float32 [4096], replicated, may hold values from -6 to 6
Outputs:
- weights: bfloat16 [4, 4096, 8192], P(None, ('gx', 'gy'), 'gz')
- checks: float32 [4, 64], replicated
The draws below stay inside these ranges and needn't reach their ends.
All inputs are finite; a program needn't handle non-finite values.
Results may differ from the reference program's by a relative error of at most 0.0029.
Values may be sent and summed in bfloat16 or wider, within the bound.
A program may use at most 256 MiB of HBM per device.

```python
import math
import jax
import jax.numpy as jnp
from jax import lax

D = 4096
FF = 8192
BLOCK = 128
SNAPS = 4
LAYERS = 4
NBLK = 64


def touch_ends(drawn, rng, low, high):
    dims = drawn.shape
    place = [jax.random.randint(jax.random.fold_in(rng, axis), (), 0, dims[axis]) for axis in range(len(dims))]
    drawn = drawn.at[tuple(place)].set(low)
    longest = dims.index(max(dims))
    place[longest] = (place[longest] + 1) % dims[longest]
    return drawn.at[tuple(place)].set(high)


def steps_of(rng, extent, cuts, low, top_value):
    gain = 1.0
    for position, parts in cuts:
        steps = jax.random.uniform(jax.random.fold_in(jax.random.fold_in(rng, 6), position), (parts,), jnp.float32, low / len(cuts), top_value / len(cuts))
        gain = gain * jnp.repeat(jnp.exp(steps), extent[position] // parts).reshape((-1,) + (1,) * (len(extent) - 1 - position))
    return gain


def normal_values(own_key, shape, scale, reach, cuts=(), kind=jnp.bfloat16):
    result = jax.random.normal(own_key, shape, jnp.float32) * scale
    if len(cuts) > 0:
        result = steps_of(own_key, shape, cuts, -0.22, 0.18) * result
    return jnp.clip(result, min=-reach, max=reach).astype(kind)


def setup_inputs(seed: int = 0) -> dict:
    streams_of = jax.random.split(jax.random.key(seed), 5)
    snapshots = normal_values(streams_of[0], (SNAPS, LAYERS, D, FF), 1.0, 6.0, ((1, 4), (2, 2), (3, 4)), jnp.float32)
    steps = touch_ends(jax.random.randint(streams_of[1], (SNAPS,), 0, 4000), jax.random.fold_in(streams_of[1], 1), 0, 3999).astype(jnp.int32)
    mask = touch_ends((jax.random.randint(streams_of[2], (LAYERS, NBLK), 0, 4) < 3).astype(jnp.int32), jax.random.fold_in(streams_of[2], 1), 0, 1)
    probe = normal_values(streams_of[3], (D,), 1.0, 6.0, (), jnp.float32)
    return {"snapshots": snapshots, "steps": steps, "mask": mask, "probe": probe}


decay_span = 1000.0

def blend_coef(steps):
    expo = jnp.exp(steps.astype(jnp.float32) / decay_span)
    return expo / jnp.sum(expo)

def block_checks(weights, probe_rows):
    per_col = jnp.einsum('d,ldc->lc', probe_rows, weights, preferred_element_type=jnp.float32, precision=lax.Precision.HIGHEST)
    layer_count = per_col.shape[0]
    grouped = per_col.reshape(layer_count, per_col.shape[1] // BLOCK, BLOCK)
    return lax.optimization_barrier(jnp.sum(grouped, axis=2)) / math.sqrt(D * BLOCK)

def reference(snapshots, steps, mask, probe):
    coef = blend_coef(steps)

    def one_layer(index):
        layer = lax.dynamic_index_in_dim(snapshots, index, 1, keepdims=False)
        acc = coef[0] * layer[0]
        for k in range(1, SNAPS):
            acc = acc + coef[k] * layer[k]
        row_mask = lax.dynamic_index_in_dim(mask, index, 0, keepdims=False)
        wide_mask = jnp.repeat(row_mask.astype(jnp.float32), BLOCK)
        weight_layer = (acc * wide_mask[None, :]).astype(jnp.bfloat16)
        return (weight_layer, block_checks(weight_layer[None], probe)[0])
    weights, checks = lax.map(one_layer, jnp.arange(LAYERS, dtype=jnp.int32))
    return (weights, checks)
```

```python
import functools
import math

import jax
import jax.numpy as jnp
from jax import lax
from jax.experimental import pallas as pl
from jax.experimental.pallas import tpu as pltpu
from jax.sharding import PartitionSpec as P

MESH = pl.DeviceIdType.MESH
BLOCK = 128
CORES = 2
CHUNK = 64
STRIP = 16
FETCH = 3
decay_span = 1000.0


def kernel(dims, snap_ref, steps_ref, mask_ref, probe_ref, land_ref, checks_ref,
           fetched, held, coef, acc, xtile, gtile,
           fetch_sem, send_sem, relay_sem, land_sem,
           xsend_sem, xland_sem, gsend_sem, gland_sem):
    nx, ny, nz, norm = dims
    snaps, _, rows, cols = snap_ref.shape
    layers = mask_ref.shape[0]
    nb = cols // BLOCK
    part = rows // ny
    chunk = fetched.shape[2]
    per = part // chunk
    steps_total = ny * per
    pairs = nz // CORES

    x = lax.axis_index("gx")
    g = lax.axis_index("gy")
    l = lax.axis_index("gz")
    me = g * nz + l
    group = ny * nz
    low = 1 - g // (ny // 2)

    def quarter(t):
        j = t % ny
        return j + low * (ny - 1 - 2 * j)

    def fetch(t):
        row = pl.multiple_of(quarter(t) * part + (t // ny) * chunk, chunk)
        slot = t % FETCH
        return pltpu.make_async_copy(
            snap_ref.at[:, 0, pl.ds(row, chunk), :], fetched.at[slot], fetch_sem.at[slot]
        )

    for t in range(min(FETCH - 1, steps_total)):
        fetch(t).start()

    barrier = pltpu.get_barrier_semaphore()

    def greet_group(i, carry):
        other = (me + i) % group
        pl.semaphore_signal(
            barrier, inc=1, device_id={"gy": other // nz, "gz": other % nz}, device_id_type=MESH
        )
        return carry

    def greet_line(i, carry):
        pl.semaphore_signal(barrier, inc=1, device_id={"gx": (x + i) % nx}, device_id_type=MESH)
        return carry

    lax.fori_loop(1, group, greet_group, 0)
    lax.fori_loop(1, nx, greet_line, 0)

    expos = [
        jnp.exp(jnp.full((1, cols), steps_ref[k], jnp.int32).astype(jnp.float32) / decay_span)
        for k in range(snaps)
    ]
    total = expos[0]
    for k in range(1, snaps):
        total = total + expos[k]
    for b in range(nb):
        keep = jnp.full((1, BLOCK), mask_ref[l, g * nb + b], jnp.int32).astype(jnp.float32)
        lanes = slice(b * BLOCK, (b + 1) * BLOCK)
        for k in range(snaps):
            coef[k, :, lanes] = (expos[k][:, lanes] / total[:, lanes]) * keep
    acc[...] = jnp.zeros_like(acc)

    pl.semaphore_wait(barrier, group - 1 + nx - 1)

    ahead = (g // CORES - l // CORES + pairs) % pairs
    final = ahead == 0
    relay_core = (l // CORES) * CORES + g % CORES
    slot_out = jnp.where(final, l, layers + CORES * (ahead - 1) + l % CORES)

    def step(t, carry):
        @pl.when(t + (FETCH - 1) < steps_total)
        def _():
            fetch(t + (FETCH - 1)).start()

        fetch(t).wait()
        slot = t % FETCH
        r = quarter(t)
        k = t // ny
        base = pl.multiple_of(k * chunk, chunk)

        def strip(i, inner):
            off = pl.multiple_of(i * STRIP, STRIP)
            here = pl.ds(off, STRIP)
            mixed = coef[0] * fetched[slot, 0, here, :]
            for s in range(1, snaps):
                mixed = mixed + coef[s] * fetched[slot, s, here, :]
            value = mixed.astype(jnp.bfloat16)
            held[r, pl.ds(pl.multiple_of(base + off, STRIP), STRIP), :] = value
            weight = probe_ref[pl.ds(pl.multiple_of(r * part + base + off, STRIP), STRIP), :]
            term = value.astype(jnp.float32) * weight
            acc[...] += term[:8] + term[8:]
            return inner

        lax.fori_loop(0, chunk // STRIP, strip, 0)

        source = held.at[r, pl.ds(base, chunk), :]
        target = land_ref.at[slot_out, pl.ds(base, chunk), :]
        stays = jnp.logical_and(r == g, relay_core == l)

        @pl.when(stays)
        def _():
            pltpu.make_async_copy(source, target, land_sem.at[slot_out, k]).start()

        @pl.when(jnp.logical_not(stays))
        def _():
            pltpu.make_async_remote_copy(
                src_ref=source,
                dst_ref=target,
                send_sem=send_sem.at[r, k],
                recv_sem=land_sem.at[slot_out, k],
                device_id={"gy": r, "gz": relay_core},
                device_id_type=MESH,
            ).start()

        return carry

    lax.fori_loop(0, steps_total, step, 0)

    def xcopy(i, slot):
        return pltpu.make_async_remote_copy(
            src_ref=xtile.at[slot],
            dst_ref=xtile.at[slot],
            send_sem=xsend_sem.at[i],
            recv_sem=xland_sem.at[slot],
            device_id={"gx": (x + i) % nx},
            device_id_type=MESH,
        )

    def gcopy(i, slot):
        other = (me + i) % group
        return pltpu.make_async_remote_copy(
            src_ref=gtile.at[slot],
            dst_ref=gtile.at[slot],
            send_sem=gsend_sem.at[i],
            recv_sem=gland_sem.at[slot],
            device_id={"gy": other // nz, "gz": other % nz},
            device_id_type=MESH,
        )

    def each(low_end, high_end, action):
        def body(i, carry):
            action(i)
            return carry

        lax.fori_loop(low_end, high_end, body, 0)

    tile = jnp.zeros(xtile.shape[1:], jnp.float32)
    row_id = lax.broadcasted_iota(jnp.int32, tile.shape, 0)
    lane_id = lax.broadcasted_iota(jnp.int32, tile.shape, 1)
    for b in range(nb):
        part_sum = jnp.sum(acc[:, b * BLOCK:(b + 1) * BLOCK], axis=(0, 1), keepdims=True)
        place = jnp.logical_and(row_id == l, lane_id == g * nb + b)
        tile = tile + jnp.where(place, part_sum, 0.0)
    xtile[x] = tile
    each(1, nx, lambda i: xcopy(i, x).start())

    def relay(ahead_by, core, k):
        goal = CORES * ((l // CORES + ahead_by) % pairs) + l % CORES
        layer = (l // CORES) * CORES + core
        slot = layers + CORES * (ahead_by - 1) + core
        here = pl.ds(pl.multiple_of(k * chunk, chunk), chunk)
        return pltpu.make_async_remote_copy(
            src_ref=land_ref.at[slot, here, :],
            dst_ref=land_ref.at[layer, here, :],
            send_sem=relay_sem.at[slot - layers, k],
            recv_sem=land_sem.at[layer, k],
            device_id={"gz": goal},
            device_id_type=MESH,
        )

    def landed(slot, k):
        here = pl.ds(pl.multiple_of(k * chunk, chunk), chunk)
        return pltpu.make_async_copy(
            land_ref.at[slot, here, :], land_ref.at[slot, here, :], land_sem.at[slot, k]
        )

    def forward(k):
        for ahead_by in range(1, pairs):
            for core in range(CORES):
                landed(layers + CORES * (ahead_by - 1) + core, k).wait()
                relay(ahead_by, core, k).start()

    half = per // 2
    each(0, half, forward)

    each(1, nx, lambda i: xcopy(i, (x + i) % nx).wait_recv())
    line = xtile[0]
    for i in range(1, nx):
        line = line + xtile[i]
    gtile[me] = line
    each(1, group, lambda i: gcopy(i, me).start())

    each(half, per, forward)

    each(1, group, lambda i: gcopy(i, (me + i) % group).wait_recv())
    whole = gtile[0]
    for i in range(1, group):
        whole = whole + gtile[i]
    checks_ref[...] = whole[: checks_ref.shape[0], : checks_ref.shape[1]] / norm

    each(1, nx, lambda i: xcopy(i, x).wait_send())
    each(1, group, lambda i: gcopy(i, me).wait_send())

    def sent(t):
        r = quarter(t)
        k = t // ny
        base = pl.multiple_of(k * chunk, chunk)

        @pl.when(jnp.logical_not(jnp.logical_and(r == g, relay_core == l)))
        def _():
            pltpu.make_async_remote_copy(
                src_ref=held.at[r, pl.ds(base, chunk), :],
                dst_ref=land_ref.at[slot_out, pl.ds(base, chunk), :],
                send_sem=send_sem.at[r, k],
                recv_sem=land_sem.at[slot_out, k],
                device_id={"gy": r, "gz": relay_core},
                device_id_type=MESH,
            ).wait_send()

    each(0, steps_total, sent)

    def relayed(k):
        for ahead_by in range(1, pairs):
            for core in range(CORES):
                relay(ahead_by, core, k).wait_send()

    each(0, per, relayed)

    def arrived(k):
        for layer in range(layers):
            landed(layer, k).wait()

    each(0, per, arrived)


def fused(nx, ny, nz, snapshots, steps, mask, probe):
    snaps, _, rows, cols = snapshots.shape
    layers, blocks = mask.shape
    part = rows // ny
    chunk = min(CHUNK, part)
    per = part // chunk
    pairs = nz // CORES
    spare = CORES * (pairs - 1)
    group = ny * nz
    tile = (-(-layers // 8) * 8, -(-blocks // BLOCK) * BLOCK)
    norm = math.sqrt(rows * nx * BLOCK)
    probe_rows = lax.dynamic_slice_in_dim(probe, lax.axis_index("gx") * rows, rows, 0)
    dma = pltpu.SemaphoreType.DMA
    land, checks = pl.pallas_call(
        functools.partial(kernel, (nx, ny, nz, norm)),
        out_shape=(
            jax.ShapeDtypeStruct((layers + spare, part, cols), jnp.bfloat16),
            jax.ShapeDtypeStruct((layers, blocks), jnp.float32),
        ),
        in_specs=[
            pl.BlockSpec(memory_space=pltpu.HBM),
            pl.BlockSpec(memory_space=pltpu.SMEM),
            pl.BlockSpec(memory_space=pltpu.SMEM),
            pl.BlockSpec(memory_space=pltpu.VMEM),
        ],
        out_specs=(
            pl.BlockSpec(memory_space=pltpu.HBM),
            pl.BlockSpec(memory_space=pltpu.VMEM),
        ),
        scratch_shapes=[
            pltpu.VMEM((FETCH, snaps, chunk, cols), jnp.float32),
            pltpu.VMEM((ny, part, cols), jnp.bfloat16),
            pltpu.VMEM((snaps, 1, cols), jnp.float32),
            pltpu.VMEM((8, cols), jnp.float32),
            pltpu.VMEM((nx,) + tile, jnp.float32),
            pltpu.VMEM((group,) + tile, jnp.float32),
            dma((FETCH,)),
            dma((ny, per)),
            dma((max(spare, 1), per)),
            dma((layers + spare, per)),
            dma((nx,)),
            dma((nx,)),
            dma((group,)),
            dma((group,)),
        ],
        compiler_params=pltpu.CompilerParams(
            collective_id=0, has_side_effects=True, vmem_limit_bytes=48 * 1024 * 1024
        ),
        cost_estimate=pl.CostEstimate(
            flops=10 * snapshots.size // snaps,
            bytes_accessed=4 * snapshots.size + 2 * layers * part * cols,
            transcendentals=0,
        ),
    )(snapshots, steps, mask, probe_rows.reshape(rows, 1))
    return land[:layers], checks


def solution(mesh):
    nx, ny, nz = (mesh.shape[name] for name in ("gx", "gy", "gz"))
    in_specs = (P(None, "gz", "gx", "gy"), P(), P(), P())
    out_specs = (P(None, ("gx", "gy"), "gz"), P())
    assert ny == nz and ny % CORES == 0
    return jax.shard_map(
        functools.partial(fused, nx, ny, nz),
        mesh=mesh, in_specs=in_specs, out_specs=out_specs, check_vma=False,
    )
```

```python
import functools
import math

import jax
import jax.numpy as jnp
from jax import lax
from jax.experimental import pallas as pl
from jax.experimental.pallas import tpu as pltpu
from jax.sharding import PartitionSpec as P

MESH = pl.DeviceIdType.MESH
BLOCK = 128
CORES = 2
CHUNK = 32
STRIP = 16
FETCH = 3
decay_span = 1000.0


def kernel(dims, snap_ref, steps_hbm, mask_hbm, probe_hbm, land_ref, checks_ref,
           fetched, held, coef, acc, xtile, gtile,
           steps_ref, mask_ref, probe_flat, probe_ref, small_sem, fetch_sem, send_sem, relay_sem, land_sem,
           xsend_sem, xland_sem, gsend_sem, gland_sem):
    nx, ny, nz, norm = dims
    snaps, _, rows, cols = snap_ref.shape
    layers = mask_hbm.shape[0]
    nb = cols // BLOCK
    part = rows // ny
    chunk = fetched.shape[2]
    per = part // chunk
    steps_total = ny * per
    pairs = nz // CORES

    x = lax.axis_index("gx")
    g = lax.axis_index("gy")
    l = lax.axis_index("gz")
    me = g * nz + l
    group = ny * nz
    low = 1 - g // (ny // 2)
    first = jnp.where(jnp.logical_or(g == 0, g == ny - 1), ny // 2, 0)

    def quarter(t):
        j = (t + first) % ny
        return j + low * (ny - 1 - 2 * j)

    def fetch(t):
        row = pl.multiple_of(quarter(t) * part + (t // ny) * chunk, chunk)
        slot = t % FETCH
        return pltpu.make_async_copy(
            snap_ref.at[:, 0, pl.ds(row, chunk), :], fetched.at[slot], fetch_sem.at[slot]
        )

    small = [
        pltpu.make_async_copy(steps_hbm, steps_ref, small_sem.at[0]),
        pltpu.make_async_copy(mask_hbm, mask_ref, small_sem.at[1]),
        pltpu.make_async_copy(probe_hbm, probe_flat, small_sem.at[2]),
    ]
    for copy in small:
        copy.start()
    for t in range(min(FETCH - 1, steps_total)):
        fetch(t).start()

    barrier = pltpu.get_barrier_semaphore()

    def greet_group(i, carry):
        other = (me + i) % group
        pl.semaphore_signal(
            barrier, inc=1, device_id={"gy": other // nz, "gz": other % nz}, device_id_type=MESH
        )
        return carry

    def greet_line(i, carry):
        pl.semaphore_signal(barrier, inc=1, device_id={"gx": (x + i) % nx}, device_id_type=MESH)
        return carry

    lax.fori_loop(1, group, greet_group, 0)
    lax.fori_loop(1, nx, greet_line, 0)

    for copy in small:
        copy.wait()
    expos = [
        jnp.exp(jnp.full((1, cols), steps_ref[k], jnp.int32).astype(jnp.float32) / decay_span)
        for k in range(snaps)
    ]
    total = expos[0]
    for k in range(1, snaps):
        total = total + expos[k]
    for b in range(nb):
        keep = jnp.full((1, BLOCK), mask_ref[l, g * nb + b], jnp.int32).astype(jnp.float32)
        lanes = slice(b * BLOCK, (b + 1) * BLOCK)
        for k in range(snaps):
            coef[k, :, lanes] = (expos[k][:, lanes] / total[:, lanes]) * keep
    acc[...] = jnp.zeros_like(acc)
    for q in range(rows // BLOCK):
        flat = probe_flat[pl.ds(x * (rows // BLOCK) + q, 1), :]
        probe_ref[q * BLOCK:(q + 1) * BLOCK, :] = jnp.broadcast_to(flat, (BLOCK, BLOCK)).T

    pl.semaphore_wait(barrier, group - 1 + nx - 1)

    ahead = (g // CORES - l // CORES + pairs) % pairs
    final = ahead == 0
    relay_core = (l // CORES) * CORES + g % CORES
    slot_out = jnp.where(final, l, layers + CORES * (ahead - 1) + l % CORES)

    def step(t, carry):
        @pl.when(t + (FETCH - 1) < steps_total)
        def _():
            fetch(t + (FETCH - 1)).start()

        fetch(t).wait()
        slot = t % FETCH
        r = quarter(t)
        k = t // ny
        base = pl.multiple_of(k * chunk, chunk)

        def strip(i, inner):
            off = pl.multiple_of(i * STRIP, STRIP)
            here = pl.ds(off, STRIP)
            mixed = coef[0] * fetched[slot, 0, here, :]
            for s in range(1, snaps):
                mixed = mixed + coef[s] * fetched[slot, s, here, :]
            value = mixed.astype(jnp.bfloat16)
            held[r, pl.ds(pl.multiple_of(base + off, STRIP), STRIP), :] = value
            weight = probe_ref[pl.ds(pl.multiple_of(r * part + base + off, STRIP), STRIP), :]
            term = value.astype(jnp.float32) * jnp.concatenate([weight] * nb, axis=1)
            acc[...] += term[:8] + term[8:]
            return inner

        lax.fori_loop(0, chunk // STRIP, strip, 0)

        source = held.at[r, pl.ds(base, chunk), :]
        target = land_ref.at[slot_out, pl.ds(base, chunk), :]
        stays = jnp.logical_and(r == g, relay_core == l)

        @pl.when(stays)
        def _():
            pltpu.make_async_copy(source, target, land_sem.at[slot_out, k]).start()

        @pl.when(jnp.logical_not(stays))
        def _():
            pltpu.make_async_remote_copy(
                src_ref=source,
                dst_ref=target,
                send_sem=send_sem.at[r, k],
                recv_sem=land_sem.at[slot_out, k],
                device_id={"gy": r, "gz": relay_core},
                device_id_type=MESH,
            ).start()

        return carry

    lax.fori_loop(0, steps_total, step, 0)

    def xcopy(i, slot):
        return pltpu.make_async_remote_copy(
            src_ref=xtile.at[slot],
            dst_ref=xtile.at[slot],
            send_sem=xsend_sem.at[i],
            recv_sem=xland_sem.at[slot],
            device_id={"gx": (x + i) % nx},
            device_id_type=MESH,
        )

    def gcopy(i, slot):
        other = (me + i) % group
        return pltpu.make_async_remote_copy(
            src_ref=gtile.at[slot],
            dst_ref=gtile.at[slot],
            send_sem=gsend_sem.at[i],
            recv_sem=gland_sem.at[slot],
            device_id={"gy": other // nz, "gz": other % nz},
            device_id_type=MESH,
        )

    def each(low_end, high_end, action):
        def body(i, carry):
            action(i)
            return carry

        lax.fori_loop(low_end, high_end, body, 0)

    tile = jnp.zeros(xtile.shape[1:], jnp.float32)
    row_id = lax.broadcasted_iota(jnp.int32, tile.shape, 0)
    lane_id = lax.broadcasted_iota(jnp.int32, tile.shape, 1)
    for b in range(nb):
        part_sum = jnp.sum(acc[:, b * BLOCK:(b + 1) * BLOCK], axis=(0, 1), keepdims=True)
        place = jnp.logical_and(row_id == l, lane_id == g * nb + b)
        tile = tile + jnp.where(place, part_sum, 0.0)
    xtile[x] = tile
    each(1, nx, lambda i: xcopy(i, x).start())

    def relay(ahead_by, core, k):
        goal = CORES * ((l // CORES + ahead_by) % pairs) + l % CORES
        layer = (l // CORES) * CORES + core
        slot = layers + CORES * (ahead_by - 1) + core
        here = pl.ds(pl.multiple_of(k * chunk, chunk), chunk)
        return pltpu.make_async_remote_copy(
            src_ref=land_ref.at[slot, here, :],
            dst_ref=land_ref.at[layer, here, :],
            send_sem=relay_sem.at[slot - layers, k],
            recv_sem=land_sem.at[layer, k],
            device_id={"gz": goal},
            device_id_type=MESH,
        )

    def landed(slot, k):
        here = pl.ds(pl.multiple_of(k * chunk, chunk), chunk)
        return pltpu.make_async_copy(
            land_ref.at[slot, here, :], land_ref.at[slot, here, :], land_sem.at[slot, k]
        )

    def forward(k):
        for ahead_by in range(1, pairs):
            for core in range(CORES):
                landed(layers + CORES * (ahead_by - 1) + core, k).wait()
                relay(ahead_by, core, k).start()

    half = per // 2
    each(0, half, forward)

    each(1, nx, lambda i: xcopy(i, (x + i) % nx).wait_recv())
    line = xtile[0]
    for i in range(1, nx):
        line = line + xtile[i]
    gtile[me] = line
    each(1, group, lambda i: gcopy(i, me).start())

    each(half, per, forward)

    each(1, group, lambda i: gcopy(i, (me + i) % group).wait_recv())
    whole = gtile[0]
    for i in range(1, group):
        whole = whole + gtile[i]
    checks_ref[...] = whole[: checks_ref.shape[0], : checks_ref.shape[1]] / norm

    each(1, nx, lambda i: xcopy(i, x).wait_send())
    each(1, group, lambda i: gcopy(i, me).wait_send())

    def sent(t):
        r = quarter(t)
        k = t // ny
        base = pl.multiple_of(k * chunk, chunk)

        @pl.when(jnp.logical_not(jnp.logical_and(r == g, relay_core == l)))
        def _():
            pltpu.make_async_remote_copy(
                src_ref=held.at[r, pl.ds(base, chunk), :],
                dst_ref=land_ref.at[slot_out, pl.ds(base, chunk), :],
                send_sem=send_sem.at[r, k],
                recv_sem=land_sem.at[slot_out, k],
                device_id={"gy": r, "gz": relay_core},
                device_id_type=MESH,
            ).wait_send()

    each(0, steps_total, sent)

    def relayed(k):
        for ahead_by in range(1, pairs):
            for core in range(CORES):
                relay(ahead_by, core, k).wait_send()

    each(0, per, relayed)

    def arrived(k):
        for layer in range(layers):
            landed(layer, k).wait()

    each(0, per, arrived)


def place(land_ref, sums_ref, weights_ref, checks_ref, sem):
    copies = [pltpu.make_async_copy(sums_ref, checks_ref, sem.at[weights_ref.shape[0]])]
    copies += [
        pltpu.make_async_copy(land_ref.at[layer], weights_ref.at[layer], sem.at[layer])
        for layer in range(weights_ref.shape[0])
    ]
    for copy in copies:
        copy.start()
    for copy in copies:
        copy.wait()


def fused(nx, ny, nz, snapshots, steps, mask, probe):
    snaps, _, rows, cols = snapshots.shape
    layers, blocks = mask.shape
    part = rows // ny
    chunk = min(CHUNK, part)
    per = part // chunk
    pairs = nz // CORES
    spare = CORES * (pairs - 1)
    group = ny * nz
    tile = (-(-layers // 8) * 8, -(-blocks // BLOCK) * BLOCK)
    norm = math.sqrt(rows * nx * BLOCK)
    dma = pltpu.SemaphoreType.DMA
    land, checks = pl.pallas_call(
        functools.partial(kernel, (nx, ny, nz, norm)),
        out_shape=(
            pltpu.VMEM((layers + spare, part, cols), jnp.bfloat16),
            pltpu.VMEM((layers, blocks), jnp.float32),
        ),
        in_specs=[
            pl.BlockSpec(memory_space=pltpu.HBM),
            pl.BlockSpec(memory_space=pltpu.HBM),
            pl.BlockSpec(memory_space=pltpu.HBM),
            pl.BlockSpec(memory_space=pltpu.HBM),
        ],
        out_specs=(
            pl.BlockSpec(memory_space=pltpu.VMEM),
            pl.BlockSpec(memory_space=pltpu.VMEM),
        ),
        scratch_shapes=[
            pltpu.VMEM((FETCH, snaps, chunk, cols), jnp.float32),
            pltpu.VMEM((ny, part, cols), jnp.bfloat16),
            pltpu.VMEM((snaps, 1, cols), jnp.float32),
            pltpu.VMEM((8, cols), jnp.float32),
            pltpu.VMEM((nx,) + tile, jnp.float32),
            pltpu.VMEM((group,) + tile, jnp.float32),
            pltpu.SMEM(steps.shape, jnp.int32),
            pltpu.SMEM(mask.shape, jnp.int32),
            pltpu.VMEM((probe.size // BLOCK, BLOCK), jnp.float32),
            pltpu.VMEM((rows, BLOCK), jnp.float32),
            dma((3,)),
            dma((FETCH,)),
            dma((ny, per)),
            dma((max(spare, 1), per)),
            dma((layers + spare, per)),
            dma((nx,)),
            dma((nx,)),
            dma((group,)),
            dma((group,)),
        ],
        compiler_params=pltpu.CompilerParams(
            collective_id=0, has_side_effects=True, vmem_limit_bytes=48 * 1024 * 1024
        ),
        cost_estimate=pl.CostEstimate(
            flops=10 * snapshots.size // snaps,
            bytes_accessed=4 * snapshots.size + 2 * layers * part * cols,
            transcendentals=0,
        ),
    )(snapshots, steps, mask, probe.reshape(-1, BLOCK))
    weights, checks = pl.pallas_call(
        place,
        out_shape=(
            jax.ShapeDtypeStruct((layers, part, cols), jnp.bfloat16),
            jax.ShapeDtypeStruct((layers, blocks), jnp.float32),
        ),
        in_specs=[pl.BlockSpec(memory_space=pltpu.VMEM)] * 2,
        out_specs=(pl.BlockSpec(memory_space=pltpu.HBM),) * 2,
        scratch_shapes=[dma((layers + 1,))],
        compiler_params=pltpu.CompilerParams(vmem_limit_bytes=24 * 1024 * 1024),
    )(land, checks)
    return weights, checks


def solution(mesh):
    nx, ny, nz = (mesh.shape[name] for name in ("gx", "gy", "gz"))
    in_specs = (P(None, "gz", "gx", "gy"), P(), P(), P())
    out_specs = (P(None, ("gx", "gy"), "gz"), P())
    assert ny == nz and ny % CORES == 0
    return jax.shard_map(
        functools.partial(fused, nx, ny, nz),
        mesh=mesh, in_specs=in_specs, out_specs=out_specs, check_vma=False,
    )
```

```python
import functools
import math

import jax
import jax.numpy as jnp
from jax import lax
from jax.experimental import pallas as pl
from jax.experimental.pallas import tpu as pltpu
from jax.sharding import PartitionSpec as P

MESH = pl.DeviceIdType.MESH
BLOCK = 128
CORES = 2
CHUNK = 32
STRIP = 16
FETCH = 3
decay_span = 1000.0


def kernel(dims, snap_ref, steps_hbm, mask_hbm, probe_hbm, land_ref, checks_ref,
           fetched, held, coef, acc, xtile, gtile,
           steps_ref, mask_ref, probe_flat, probe_ref, small_sem, fetch_sem, send_sem, relay_sem, land_sem,
           xsend_sem, xland_sem, gsend_sem, gland_sem):
    nx, ny, nz, norm = dims
    snaps, _, rows, cols = snap_ref.shape
    layers = mask_hbm.shape[0]
    nb = cols // BLOCK
    part = rows // ny
    chunk = fetched.shape[2]
    per = part // chunk
    steps_total = ny * per
    pairs = nz // CORES

    x = lax.axis_index("gx")
    g = lax.axis_index("gy")
    l = lax.axis_index("gz")
    me = g * nz + l
    group = ny * nz
    low = 1 - g // (ny // 2)
    edge = jnp.logical_or(g == 0, g == ny - 1)
    across = ny // 2
    near = ny - 1 - across
    near_end = near * per
    across_end = near_end + across * per

    def place_of(t):
        wide = max(near, 1)
        later = t - near_end
        in_near = t < near_end
        in_across = t < across_end
        edge_j = jnp.where(
            in_near, across + t % wide, jnp.where(in_across, later % across, ny - 1)
        )
        edge_k = jnp.where(
            in_near, t // wide, jnp.where(in_across, later // across, t - across_end)
        )
        j = jnp.where(edge, edge_j, t % ny)
        k = jnp.where(edge, edge_k, t // ny)
        return j + low * (ny - 1 - 2 * j), k

    def fetch(t):
        r, k = place_of(t)
        row = pl.multiple_of(r * part + k * chunk, chunk)
        slot = t % FETCH
        return pltpu.make_async_copy(
            snap_ref.at[:, 0, pl.ds(row, chunk), :], fetched.at[slot], fetch_sem.at[slot]
        )

    small = [
        pltpu.make_async_copy(steps_hbm, steps_ref, small_sem.at[0]),
        pltpu.make_async_copy(mask_hbm, mask_ref, small_sem.at[1]),
        pltpu.make_async_copy(probe_hbm, probe_flat, small_sem.at[2]),
    ]
    for copy in small:
        copy.start()
    for t in range(min(FETCH - 1, steps_total)):
        fetch(t).start()

    barrier = pltpu.get_barrier_semaphore()

    def greet_group(i, carry):
        other = (me + i) % group
        pl.semaphore_signal(
            barrier, inc=1, device_id={"gy": other // nz, "gz": other % nz}, device_id_type=MESH
        )
        return carry

    def greet_line(i, carry):
        pl.semaphore_signal(barrier, inc=1, device_id={"gx": (x + i) % nx}, device_id_type=MESH)
        return carry

    lax.fori_loop(1, group, greet_group, 0)
    lax.fori_loop(1, nx, greet_line, 0)

    for copy in small:
        copy.wait()
    expos = [
        jnp.exp(jnp.full((1, cols), steps_ref[k], jnp.int32).astype(jnp.float32) / decay_span)
        for k in range(snaps)
    ]
    total = expos[0]
    for k in range(1, snaps):
        total = total + expos[k]
    for b in range(nb):
        keep = jnp.full((1, BLOCK), mask_ref[l, g * nb + b], jnp.int32).astype(jnp.float32)
        lanes = slice(b * BLOCK, (b + 1) * BLOCK)
        for k in range(snaps):
            coef[k, :, lanes] = (expos[k][:, lanes] / total[:, lanes]) * keep
    acc[...] = jnp.zeros_like(acc)
    for q in range(rows // BLOCK):
        flat = probe_flat[pl.ds(x * (rows // BLOCK) + q, 1), :]
        probe_ref[q * BLOCK:(q + 1) * BLOCK, :] = jnp.broadcast_to(flat, (BLOCK, BLOCK)).T

    pl.semaphore_wait(barrier, group - 1 + nx - 1)

    ahead = (g // CORES - l // CORES + pairs) % pairs
    final = ahead == 0
    relay_core = (l // CORES) * CORES + g % CORES
    slot_out = jnp.where(final, l, layers + CORES * (ahead - 1) + l % CORES)

    def step(t, carry):
        @pl.when(t + (FETCH - 1) < steps_total)
        def _():
            fetch(t + (FETCH - 1)).start()

        fetch(t).wait()
        slot = t % FETCH
        r, k = place_of(t)
        base = pl.multiple_of(k * chunk, chunk)

        def strip(i, inner):
            off = pl.multiple_of(i * STRIP, STRIP)
            here = pl.ds(off, STRIP)
            mixed = coef[0] * fetched[slot, 0, here, :]
            for s in range(1, snaps):
                mixed = mixed + coef[s] * fetched[slot, s, here, :]
            value = mixed.astype(jnp.bfloat16)
            held[r, pl.ds(pl.multiple_of(base + off, STRIP), STRIP), :] = value
            weight = probe_ref[pl.ds(pl.multiple_of(r * part + base + off, STRIP), STRIP), :]
            term = value.astype(jnp.float32) * jnp.concatenate([weight] * nb, axis=1)
            acc[...] += term[:8] + term[8:]
            return inner

        lax.fori_loop(0, chunk // STRIP, strip, 0)

        source = held.at[r, pl.ds(base, chunk), :]
        target = land_ref.at[slot_out, pl.ds(base, chunk), :]
        stays = jnp.logical_and(r == g, relay_core == l)

        @pl.when(stays)
        def _():
            pltpu.make_async_copy(source, target, land_sem.at[slot_out, k]).start()

        @pl.when(jnp.logical_not(stays))
        def _():
            pltpu.make_async_remote_copy(
                src_ref=source,
                dst_ref=target,
                send_sem=send_sem.at[r, k],
                recv_sem=land_sem.at[slot_out, k],
                device_id={"gy": r, "gz": relay_core},
                device_id_type=MESH,
            ).start()

        return carry

    lax.fori_loop(0, steps_total, step, 0)

    def xcopy(i, slot):
        return pltpu.make_async_remote_copy(
            src_ref=xtile.at[slot],
            dst_ref=xtile.at[slot],
            send_sem=xsend_sem.at[i],
            recv_sem=xland_sem.at[slot],
            device_id={"gx": (x + i) % nx},
            device_id_type=MESH,
        )

    def gcopy(i, slot):
        other = (me + i) % group
        return pltpu.make_async_remote_copy(
            src_ref=gtile.at[slot],
            dst_ref=gtile.at[slot],
            send_sem=gsend_sem.at[i],
            recv_sem=gland_sem.at[slot],
            device_id={"gy": other // nz, "gz": other % nz},
            device_id_type=MESH,
        )

    def each(low_end, high_end, action):
        def body(i, carry):
            action(i)
            return carry

        lax.fori_loop(low_end, high_end, body, 0)

    tile = jnp.zeros(xtile.shape[1:], jnp.float32)
    row_id = lax.broadcasted_iota(jnp.int32, tile.shape, 0)
    lane_id = lax.broadcasted_iota(jnp.int32, tile.shape, 1)
    for b in range(nb):
        part_sum = jnp.sum(acc[:, b * BLOCK:(b + 1) * BLOCK], axis=(0, 1), keepdims=True)
        place = jnp.logical_and(row_id == l, lane_id == g * nb + b)
        tile = tile + jnp.where(place, part_sum, 0.0)
    xtile[x] = tile
    each(1, nx, lambda i: xcopy(i, x).start())

    def relay(ahead_by, core, k):
        goal = CORES * ((l // CORES + ahead_by) % pairs) + l % CORES
        layer = (l // CORES) * CORES + core
        slot = layers + CORES * (ahead_by - 1) + core
        here = pl.ds(pl.multiple_of(k * chunk, chunk), chunk)
        return pltpu.make_async_remote_copy(
            src_ref=land_ref.at[slot, here, :],
            dst_ref=land_ref.at[layer, here, :],
            send_sem=relay_sem.at[slot - layers, k],
            recv_sem=land_sem.at[layer, k],
            device_id={"gz": goal},
            device_id_type=MESH,
        )

    def landed(slot, k):
        here = pl.ds(pl.multiple_of(k * chunk, chunk), chunk)
        return pltpu.make_async_copy(
            land_ref.at[slot, here, :], land_ref.at[slot, here, :], land_sem.at[slot, k]
        )

    def forward(k):
        for ahead_by in range(1, pairs):
            for core in range(CORES):
                landed(layers + CORES * (ahead_by - 1) + core, k).wait()
                relay(ahead_by, core, k).start()

    half = per // 2
    each(0, half, forward)

    each(1, nx, lambda i: xcopy(i, (x + i) % nx).wait_recv())
    line = xtile[0]
    for i in range(1, nx):
        line = line + xtile[i]
    gtile[me] = line
    each(1, group, lambda i: gcopy(i, me).start())

    each(half, per, forward)

    each(1, group, lambda i: gcopy(i, (me + i) % group).wait_recv())
    whole = gtile[0]
    for i in range(1, group):
        whole = whole + gtile[i]
    checks_ref[...] = whole[: checks_ref.shape[0], : checks_ref.shape[1]] / norm

    each(1, nx, lambda i: xcopy(i, x).wait_send())
    each(1, group, lambda i: gcopy(i, me).wait_send())

    def sent(t):
        r, k = place_of(t)
        base = pl.multiple_of(k * chunk, chunk)

        @pl.when(jnp.logical_not(jnp.logical_and(r == g, relay_core == l)))
        def _():
            pltpu.make_async_remote_copy(
                src_ref=held.at[r, pl.ds(base, chunk), :],
                dst_ref=land_ref.at[slot_out, pl.ds(base, chunk), :],
                send_sem=send_sem.at[r, k],
                recv_sem=land_sem.at[slot_out, k],
                device_id={"gy": r, "gz": relay_core},
                device_id_type=MESH,
            ).wait_send()

    each(0, steps_total, sent)

    def relayed(k):
        for ahead_by in range(1, pairs):
            for core in range(CORES):
                relay(ahead_by, core, k).wait_send()

    each(0, per, relayed)

    def arrived(k):
        for layer in range(layers):
            landed(layer, k).wait()

    each(0, per, arrived)


def place(land_ref, sums_ref, weights_ref, checks_ref, sem):
    copies = [pltpu.make_async_copy(sums_ref, checks_ref, sem.at[weights_ref.shape[0]])]
    copies += [
        pltpu.make_async_copy(land_ref.at[layer], weights_ref.at[layer], sem.at[layer])
        for layer in range(weights_ref.shape[0])
    ]
    for copy in copies:
        copy.start()
    for copy in copies:
        copy.wait()


def fused(nx, ny, nz, snapshots, steps, mask, probe):
    snaps, _, rows, cols = snapshots.shape
    layers, blocks = mask.shape
    part = rows // ny
    chunk = min(CHUNK, part)
    per = part // chunk
    pairs = nz // CORES
    spare = CORES * (pairs - 1)
    group = ny * nz
    tile = (-(-layers // 8) * 8, -(-blocks // BLOCK) * BLOCK)
    norm = math.sqrt(rows * nx * BLOCK)
    dma = pltpu.SemaphoreType.DMA
    land, checks = pl.pallas_call(
        functools.partial(kernel, (nx, ny, nz, norm)),
        out_shape=(
            pltpu.VMEM((layers + spare, part, cols), jnp.bfloat16),
            pltpu.VMEM((layers, blocks), jnp.float32),
        ),
        in_specs=[
            pl.BlockSpec(memory_space=pltpu.HBM),
            pl.BlockSpec(memory_space=pltpu.HBM),
            pl.BlockSpec(memory_space=pltpu.HBM),
            pl.BlockSpec(memory_space=pltpu.HBM),
        ],
        out_specs=(
            pl.BlockSpec(memory_space=pltpu.VMEM),
            pl.BlockSpec(memory_space=pltpu.VMEM),
        ),
        scratch_shapes=[
            pltpu.VMEM((FETCH, snaps, chunk, cols), jnp.float32),
            pltpu.VMEM((ny, part, cols), jnp.bfloat16),
            pltpu.VMEM((snaps, 1, cols), jnp.float32),
            pltpu.VMEM((8, cols), jnp.float32),
            pltpu.VMEM((nx,) + tile, jnp.float32),
            pltpu.VMEM((group,) + tile, jnp.float32),
            pltpu.SMEM(steps.shape, jnp.int32),
            pltpu.SMEM(mask.shape, jnp.int32),
            pltpu.VMEM((probe.size // BLOCK, BLOCK), jnp.float32),
            pltpu.VMEM((rows, BLOCK), jnp.float32),
            dma((3,)),
            dma((FETCH,)),
            dma((ny, per)),
            dma((max(spare, 1), per)),
            dma((layers + spare, per)),
            dma((nx,)),
            dma((nx,)),
            dma((group,)),
            dma((group,)),
        ],
        compiler_params=pltpu.CompilerParams(
            collective_id=0, has_side_effects=True, vmem_limit_bytes=48 * 1024 * 1024
        ),
        cost_estimate=pl.CostEstimate(
            flops=10 * snapshots.size // snaps,
            bytes_accessed=4 * snapshots.size + 2 * layers * part * cols,
            transcendentals=0,
        ),
    )(snapshots, steps, mask, probe.reshape(-1, BLOCK))
    weights, checks = pl.pallas_call(
        place,
        out_shape=(
            jax.ShapeDtypeStruct((layers, part, cols), jnp.bfloat16),
            jax.ShapeDtypeStruct((layers, blocks), jnp.float32),
        ),
        in_specs=[pl.BlockSpec(memory_space=pltpu.VMEM)] * 2,
        out_specs=(pl.BlockSpec(memory_space=pltpu.HBM),) * 2,
        scratch_shapes=[dma((layers + 1,))],
        compiler_params=pltpu.CompilerParams(vmem_limit_bytes=24 * 1024 * 1024),
    )(land, checks)
    return weights, checks


def solution(mesh):
    nx, ny, nz = (mesh.shape[name] for name in ("gx", "gy", "gz"))
    in_specs = (P(None, "gz", "gx", "gy"), P(), P(), P())
    out_specs = (P(None, ("gx", "gy"), "gz"), P())
    assert ny == nz and ny % CORES == 0
    return jax.shard_map(
        functools.partial(fused, nx, ny, nz),
        mesh=mesh, in_specs=in_specs, out_specs=out_specs, check_vma=False,
    )
```

```python
import functools
import math

import jax
import jax.numpy as jnp
from jax import lax
from jax.experimental import pallas as pl
from jax.experimental.pallas import tpu as pltpu
from jax.sharding import PartitionSpec as P

MESH = pl.DeviceIdType.MESH
BLOCK = 128
CORES = 2
CHUNK = 16
STRIP = 16
FETCH = 4
decay_span = 1000.0


def kernel(dims, snap_ref, steps_hbm, mask_hbm, probe_hbm, land_ref, checks_ref,
           fetched, held, coef, acc, xtile, gtile,
           steps_ref, mask_ref, probe_flat, probe_ref, small_sem, fetch_sem, send_sem, relay_sem, land_sem,
           xsend_sem, xland_sem, gsend_sem, gland_sem):
    nx, ny, nz, norm = dims
    snaps, _, rows, cols = snap_ref.shape
    layers = mask_hbm.shape[0]
    nb = cols // BLOCK
    part = rows // ny
    chunk = fetched.shape[2]
    per = part // chunk
    steps_total = ny * per
    pairs = nz // CORES

    x = lax.axis_index("gx")
    g = lax.axis_index("gy")
    l = lax.axis_index("gz")
    me = g * nz + l
    group = ny * nz
    low = 1 - g // (ny // 2)
    first = jnp.where(jnp.logical_or(g == 0, g == ny - 1), ny // 2, 0)

    def quarter(t):
        j = (t + first) % ny
        return j + low * (ny - 1 - 2 * j)

    def fetch(t):
        row = pl.multiple_of(quarter(t) * part + (t // ny) * chunk, chunk)
        slot = t % FETCH
        return pltpu.make_async_copy(
            snap_ref.at[:, 0, pl.ds(row, chunk), :], fetched.at[slot], fetch_sem.at[slot]
        )

    small = [
        pltpu.make_async_copy(steps_hbm, steps_ref, small_sem.at[0]),
        pltpu.make_async_copy(mask_hbm, mask_ref, small_sem.at[1]),
        pltpu.make_async_copy(probe_hbm, probe_flat, small_sem.at[2]),
    ]
    for copy in small:
        copy.start()
    for t in range(min(FETCH - 1, steps_total)):
        fetch(t).start()

    barrier = pltpu.get_barrier_semaphore()

    def greet_group(i, carry):
        other = (me + i) % group
        pl.semaphore_signal(
            barrier, inc=1, device_id={"gy": other // nz, "gz": other % nz}, device_id_type=MESH
        )
        return carry

    def greet_line(i, carry):
        pl.semaphore_signal(barrier, inc=1, device_id={"gx": (x + i) % nx}, device_id_type=MESH)
        return carry

    lax.fori_loop(1, group, greet_group, 0)
    lax.fori_loop(1, nx, greet_line, 0)

    for copy in small:
        copy.wait()
    expos = [
        jnp.exp(jnp.full((1, cols), steps_ref[k], jnp.int32).astype(jnp.float32) / decay_span)
        for k in range(snaps)
    ]
    total = expos[0]
    for k in range(1, snaps):
        total = total + expos[k]
    for b in range(nb):
        keep = jnp.full((1, BLOCK), mask_ref[l, g * nb + b], jnp.int32).astype(jnp.float32)
        lanes = slice(b * BLOCK, (b + 1) * BLOCK)
        for k in range(snaps):
            coef[k, :, lanes] = (expos[k][:, lanes] / total[:, lanes]) * keep
    acc[...] = jnp.zeros_like(acc)
    for q in range(rows // BLOCK):
        flat = probe_flat[pl.ds(x * (rows // BLOCK) + q, 1), :]
        probe_ref[q * BLOCK:(q + 1) * BLOCK, :] = jnp.broadcast_to(flat, (BLOCK, BLOCK)).T

    pl.semaphore_wait(barrier, group - 1 + nx - 1)

    ahead = (g // CORES - l // CORES + pairs) % pairs
    final = ahead == 0
    relay_core = (l // CORES) * CORES + g % CORES
    slot_out = jnp.where(final, l, layers + CORES * (ahead - 1) + l % CORES)

    def step(t, carry):
        @pl.when(t + (FETCH - 1) < steps_total)
        def _():
            fetch(t + (FETCH - 1)).start()

        fetch(t).wait()
        slot = t % FETCH
        r = quarter(t)
        k = t // ny
        base = pl.multiple_of(k * chunk, chunk)

        def strip(i, inner):
            off = pl.multiple_of(i * STRIP, STRIP)
            here = pl.ds(off, STRIP)
            mixed = coef[0] * fetched[slot, 0, here, :]
            for s in range(1, snaps):
                mixed = mixed + coef[s] * fetched[slot, s, here, :]
            value = mixed.astype(jnp.bfloat16)
            held[r, pl.ds(pl.multiple_of(base + off, STRIP), STRIP), :] = value
            weight = probe_ref[pl.ds(pl.multiple_of(r * part + base + off, STRIP), STRIP), :]
            term = value.astype(jnp.float32) * jnp.concatenate([weight] * nb, axis=1)
            acc[...] += term[:8] + term[8:]
            return inner

        lax.fori_loop(0, chunk // STRIP, strip, 0)

        source = held.at[r, pl.ds(base, chunk), :]
        target = land_ref.at[slot_out, pl.ds(base, chunk), :]
        stays = jnp.logical_and(r == g, relay_core == l)

        @pl.when(stays)
        def _():
            pltpu.make_async_copy(source, target, land_sem.at[slot_out, k]).start()

        @pl.when(jnp.logical_not(stays))
        def _():
            pltpu.make_async_remote_copy(
                src_ref=source,
                dst_ref=target,
                send_sem=send_sem.at[r, k],
                recv_sem=land_sem.at[slot_out, k],
                device_id={"gy": r, "gz": relay_core},
                device_id_type=MESH,
            ).start()

        return carry

    lax.fori_loop(0, steps_total, step, 0)

    def xcopy(i, slot):
        return pltpu.make_async_remote_copy(
            src_ref=xtile.at[slot],
            dst_ref=xtile.at[slot],
            send_sem=xsend_sem.at[i],
            recv_sem=xland_sem.at[slot],
            device_id={"gx": (x + i) % nx},
            device_id_type=MESH,
        )

    def gcopy(i, slot):
        other = (me + i) % group
        return pltpu.make_async_remote_copy(
            src_ref=gtile.at[slot],
            dst_ref=gtile.at[slot],
            send_sem=gsend_sem.at[i],
            recv_sem=gland_sem.at[slot],
            device_id={"gy": other // nz, "gz": other % nz},
            device_id_type=MESH,
        )

    def each(low_end, high_end, action):
        def body(i, carry):
            action(i)
            return carry

        lax.fori_loop(low_end, high_end, body, 0)

    tile = jnp.zeros(xtile.shape[1:], jnp.float32)
    row_id = lax.broadcasted_iota(jnp.int32, tile.shape, 0)
    lane_id = lax.broadcasted_iota(jnp.int32, tile.shape, 1)
    for b in range(nb):
        part_sum = jnp.sum(acc[:, b * BLOCK:(b + 1) * BLOCK], axis=(0, 1), keepdims=True)
        place = jnp.logical_and(row_id == l, lane_id == g * nb + b)
        tile = tile + jnp.where(place, part_sum, 0.0)
    xtile[x] = tile
    each(1, nx, lambda i: xcopy(i, x).start())

    def relay(ahead_by, core, k):
        goal = CORES * ((l // CORES + ahead_by) % pairs) + l % CORES
        layer = (l // CORES) * CORES + core
        slot = layers + CORES * (ahead_by - 1) + core
        here = pl.ds(pl.multiple_of(k * chunk, chunk), chunk)
        return pltpu.make_async_remote_copy(
            src_ref=land_ref.at[slot, here, :],
            dst_ref=land_ref.at[layer, here, :],
            send_sem=relay_sem.at[slot - layers, k],
            recv_sem=land_sem.at[layer, k],
            device_id={"gz": goal},
            device_id_type=MESH,
        )

    def landed(slot, k):
        here = pl.ds(pl.multiple_of(k * chunk, chunk), chunk)
        return pltpu.make_async_copy(
            land_ref.at[slot, here, :], land_ref.at[slot, here, :], land_sem.at[slot, k]
        )

    def forward(k):
        for ahead_by in range(1, pairs):
            for core in range(CORES):
                landed(layers + CORES * (ahead_by - 1) + core, k).wait()
                relay(ahead_by, core, k).start()

    half = per // 2
    each(0, half, forward)

    each(1, nx, lambda i: xcopy(i, (x + i) % nx).wait_recv())
    line = xtile[0]
    for i in range(1, nx):
        line = line + xtile[i]
    gtile[me] = line
    each(1, group, lambda i: gcopy(i, me).start())

    each(half, per, forward)

    each(1, group, lambda i: gcopy(i, (me + i) % group).wait_recv())
    whole = gtile[0]
    for i in range(1, group):
        whole = whole + gtile[i]
    checks_ref[...] = whole[: checks_ref.shape[0], : checks_ref.shape[1]] / norm

    each(1, nx, lambda i: xcopy(i, x).wait_send())
    each(1, group, lambda i: gcopy(i, me).wait_send())

    def sent(t):
        r = quarter(t)
        k = t // ny
        base = pl.multiple_of(k * chunk, chunk)

        @pl.when(jnp.logical_not(jnp.logical_and(r == g, relay_core == l)))
        def _():
            pltpu.make_async_remote_copy(
                src_ref=held.at[r, pl.ds(base, chunk), :],
                dst_ref=land_ref.at[slot_out, pl.ds(base, chunk), :],
                send_sem=send_sem.at[r, k],
                recv_sem=land_sem.at[slot_out, k],
                device_id={"gy": r, "gz": relay_core},
                device_id_type=MESH,
            ).wait_send()

    each(0, steps_total, sent)

    def relayed(k):
        for ahead_by in range(1, pairs):
            for core in range(CORES):
                relay(ahead_by, core, k).wait_send()

    each(0, per, relayed)

    def arrived(k):
        for layer in range(layers):
            landed(layer, k).wait()

    each(0, per, arrived)


def place(land_ref, sums_ref, weights_ref, checks_ref, sem):
    copies = [pltpu.make_async_copy(sums_ref, checks_ref, sem.at[weights_ref.shape[0]])]
    copies += [
        pltpu.make_async_copy(land_ref.at[layer], weights_ref.at[layer], sem.at[layer])
        for layer in range(weights_ref.shape[0])
    ]
    for copy in copies:
        copy.start()
    for copy in copies:
        copy.wait()


def fused(nx, ny, nz, snapshots, steps, mask, probe):
    snaps, _, rows, cols = snapshots.shape
    layers, blocks = mask.shape
    part = rows // ny
    chunk = min(CHUNK, part)
    per = part // chunk
    pairs = nz // CORES
    spare = CORES * (pairs - 1)
    group = ny * nz
    tile = (-(-layers // 8) * 8, -(-blocks // BLOCK) * BLOCK)
    norm = math.sqrt(rows * nx * BLOCK)
    dma = pltpu.SemaphoreType.DMA
    land, checks = pl.pallas_call(
        functools.partial(kernel, (nx, ny, nz, norm)),
        out_shape=(
            pltpu.VMEM((layers + spare, part, cols), jnp.bfloat16),
            pltpu.VMEM((layers, blocks), jnp.float32),
        ),
        in_specs=[
            pl.BlockSpec(memory_space=pltpu.HBM),
            pl.BlockSpec(memory_space=pltpu.HBM),
            pl.BlockSpec(memory_space=pltpu.HBM),
            pl.BlockSpec(memory_space=pltpu.HBM),
        ],
        out_specs=(
            pl.BlockSpec(memory_space=pltpu.VMEM),
            pl.BlockSpec(memory_space=pltpu.VMEM),
        ),
        scratch_shapes=[
            pltpu.VMEM((FETCH, snaps, chunk, cols), jnp.float32),
            pltpu.VMEM((ny, part, cols), jnp.bfloat16),
            pltpu.VMEM((snaps, 1, cols), jnp.float32),
            pltpu.VMEM((8, cols), jnp.float32),
            pltpu.VMEM((nx,) + tile, jnp.float32),
            pltpu.VMEM((group,) + tile, jnp.float32),
            pltpu.SMEM(steps.shape, jnp.int32),
            pltpu.SMEM(mask.shape, jnp.int32),
            pltpu.VMEM((probe.size // BLOCK, BLOCK), jnp.float32),
            pltpu.VMEM((rows, BLOCK), jnp.float32),
            dma((3,)),
            dma((FETCH,)),
            dma((ny, per)),
            dma((max(spare, 1), per)),
            dma((layers + spare, per)),
            dma((nx,)),
            dma((nx,)),
            dma((group,)),
            dma((group,)),
        ],
        compiler_params=pltpu.CompilerParams(
            collective_id=0, has_side_effects=True, vmem_limit_bytes=48 * 1024 * 1024
        ),
        cost_estimate=pl.CostEstimate(
            flops=10 * snapshots.size // snaps,
            bytes_accessed=4 * snapshots.size + 2 * layers * part * cols,
            transcendentals=0,
        ),
    )(snapshots, steps, mask, probe.reshape(-1, BLOCK))
    weights, checks = pl.pallas_call(
        place,
        out_shape=(
            jax.ShapeDtypeStruct((layers, part, cols), jnp.bfloat16),
            jax.ShapeDtypeStruct((layers, blocks), jnp.float32),
        ),
        in_specs=[pl.BlockSpec(memory_space=pltpu.VMEM)] * 2,
        out_specs=(pl.BlockSpec(memory_space=pltpu.HBM),) * 2,
        scratch_shapes=[dma((layers + 1,))],
        compiler_params=pltpu.CompilerParams(vmem_limit_bytes=24 * 1024 * 1024),
    )(land, checks)
    return weights, checks


def solution(mesh):
    nx, ny, nz = (mesh.shape[name] for name in ("gx", "gy", "gz"))
    in_specs = (P(None, "gz", "gx", "gy"), P(), P(), P())
    out_specs = (P(None, ("gx", "gy"), "gz"), P())
    assert ny == nz and ny % CORES == 0
    return jax.shard_map(
        functools.partial(fused, nx, ny, nz),
        mesh=mesh, in_specs=in_specs, out_specs=out_specs, check_vma=False,
    )
```
